256 devices in a mesh: expert: 64 (over z, x, core), dp: 4 (over y).
Axes of the slice: x: 4, y: 4, z: 8, core: 2. Of those that a mesh axis runs over, the one named last changes fastest.
Arguments:
- tokens: bfloat16 [8, 4096, 2560], P('dp', 'expert'), may hold values from -6 to 6
- out_grad: bfloat16 [8, 4096, 2560], P('dp', 'expert'), may hold values from -6 to 6
- steps_ids: int32 [8], P('dp'), may hold values from 0 to 999
- ada_weight: bfloat16 [256, 7680], replicated, may hold values from -0.375 to 0.375
- router_weight: bfloat16 [2560, 64], replicated, may hold values from -0.125 to 0.125
- w_in: bfloat16 [64, 2560, 1280], P('expert', 'dp'), may hold values from -0.125 to 0.125
- w_out: bfloat16 [64, 1280, 2560], P('expert', 'dp'), may hold values from -0.15625 to 0.15625
- chosen: int32 [64, 8, 128], P(None, 'dp'), may hold values from 0 to 4095, as said below
Outputs:
- d_tokens: bfloat16 [8, 4096, 2560], P('dp', 'expert')
- d_modulation: float32 [8, 7680], P('dp')
- dw_in: bfloat16 [64, 2560, 1280], P('expert', 'dp')
- dw_out: bfloat16 [64, 1280, 2560], P('expert', 'dp')
The draws below stay inside these ranges and needn't reach their ends.
Inputs may be any that keep to these rules, and one draw needn't show every extreme that they name: `chosen`: for each expert and image the 128 tokens are distinct; at most 6 of them lie in any one device's block of 64 consecutive tokens, and exactly 6 in some block.
All inputs are finite; a program needn't handle non-finite values.
Results may differ from the reference program's by a relative error of at most 0.022.
Values may be sent and summed in bfloat16 or wider, within the bound.
No kernel may reach another device: no remote copies, remote signals or barrier semaphores. Data moves between devices by JAX's collectives and lax.ppermute only.
A program may use at most 128 MiB of HBM per device.

```python
import math
import jax
import jax.numpy as jnp
from jax import lax

D = 2560
FF = 1280
FREQ = 256
TOK_DEV = 64
EXPERTS = 64
SEQLEN = 4096
IMAGES = 8
CAP = 128
MOST = 6
N_DP = 4


def draw_chosen(key, part):
    key = jax.random.fold_in(key, 11)
    sources = SEQLEN // TOK_DEV
    candidates = sources * MOST

    def pick_one(one_key):
        key_hot, key_score, key_perm = jax.random.split(one_key, 3)
        hot_source = jax.random.randint(key_hot, (), 0, sources)
        slot_ids = jnp.arange(candidates, dtype=jnp.int32)
        scores = jax.random.randint(key_score, (candidates,), 0, 1 << 20) * candidates + slot_ids
        scores = jnp.where(slot_ids // MOST == hot_source, slot_ids - candidates, scores)
        picked = jnp.argsort(scores)[:CAP].astype(jnp.int32)
        source_dev = picked // MOST
        within = picked % MOST
        perm_scores = jax.random.randint(key_perm, (sources, TOK_DEV), 0, 1 << 20) * TOK_DEV + jnp.arange(TOK_DEV, dtype=jnp.int32)[None, :]
        placing = jnp.argsort(perm_scores, axis=1).astype(jnp.int32)
        return (source_dev * TOK_DEV + placing[source_dev, within]).astype(jnp.int32)
    key_list = jax.random.split(key, EXPERTS * IMAGES)
    return jax.vmap(pick_one)(key_list).reshape(EXPERTS, IMAGES, CAP)


def with_ends(entries, rng, smallest, top_value):
    longest = entries.shape.index(max(entries.shape))
    spots = []
    for shift in (0, 1):
        where = [jax.random.randint(jax.random.fold_in(rng, axis), (), 0, length) for axis, length in enumerate(entries.shape)]
        where[longest] = (where[longest] + shift) % entries.shape[longest]
        spots.append(tuple(where))
    return entries.at[spots[0]].set(smallest).at[spots[1]].set(top_value)


def level_of(own_key, shape, cuts, smallest, largest):
    gain, own = 1.0, jax.random.fold_in(own_key, 6)
    for axis_at, shards_of in cuts:
        heights = jnp.exp(jax.random.uniform(jax.random.fold_in(own, axis_at), (shards_of,), jnp.float32, smallest / len(cuts), largest / len(cuts)))
        gain = gain * jnp.repeat(heights, shape[axis_at] // shards_of).reshape([-1 if axis == axis_at else 1 for axis in range(len(shape))])
    return gain


def noise(stream_key, dims, width, most, cuts=(), kind=jnp.bfloat16):
    factor_of = level_of(stream_key, dims, cuts, -0.22, 0.18) if cuts else 1.0
    result = jax.random.normal(stream_key, dims, jnp.float32) * width * factor_of
    return jnp.minimum(jnp.maximum(result, -most), most).astype(kind)


def setup_inputs(seed: int = 0) -> dict:
    seeds = jax.random.split(jax.random.key(seed), 9)
    tokens = noise(seeds[0], (IMAGES, SEQLEN, D), 1.0, 6.0, ((0, 4), (1, 64)))
    out_grad = noise(seeds[1], (IMAGES, SEQLEN, D), 1.0, 6.0, ((0, 4), (1, 64)))
    steps_ids = with_ends(jax.random.randint(seeds[2], (IMAGES,), 0, 1000), jax.random.fold_in(seeds[2], 1), 0, 999).astype(jnp.int32)
    ada_weight = noise(seeds[3], (FREQ, 3 * D), FREQ ** -0.5, 0.375)
    router_weight = noise(seeds[4], (D, EXPERTS), D ** -0.5, 0.125)
    w_in = noise(seeds[5], (EXPERTS, D, FF), D ** -0.5, 0.125, ((0, 64), (1, 4)))
    w_out = noise(seeds[6], (EXPERTS, FF, D), FF ** -0.5, 0.15625, ((0, 64), (1, 4)))
    chosen = draw_chosen(jax.random.fold_in(seeds[8], 71), 0)
    return dict(tokens=tokens, out_grad=out_grad, steps_ids=steps_ids, ada_weight=ada_weight, router_weight=router_weight, w_in=w_in, w_out=w_out, chosen=chosen)


GELU_K = math.sqrt(2.0 / math.pi)
GELU_C = 0.044715
LAYER_EPS = 1e-06

def gelu_pair(preact):
    inner_arg = GELU_K * (preact + GELU_C * preact * preact * preact)
    tangent = jnp.tanh(inner_arg)
    gelu_value = 0.5 * preact * (1.0 + tangent)
    gelu_slope = 0.5 * (1.0 + tangent) + 0.5 * preact * (1.0 - tangent * tangent) * GELU_K * (1.0 + 3.0 * GELU_C * preact * preact)
    return (gelu_value, gelu_slope)

def time_features(steps_ids, feature_count):
    half_width = feature_count // 2
    frequencies = jnp.exp(-math.log(10000.0) * jnp.arange(half_width, dtype=jnp.float32) / half_width)
    angles = steps_ids.astype(jnp.float32)[:, None] * frequencies[None, :]
    features = jnp.concatenate([jnp.cos(angles), jnp.sin(angles)], axis=1)
    return jax.nn.silu(features).astype(jnp.bfloat16)

def modulation_parts(steps_ids, ada_weight, model_width):
    modulation = jnp.dot(time_features(steps_ids, ada_weight.shape[0]), ada_weight, preferred_element_type=jnp.float32)
    shift_part = modulation[:, None, :model_width]
    scale_part = modulation[:, None, model_width:2 * model_width]
    gate_vec = modulation[:, None, 2 * model_width:]
    return (shift_part, scale_part, gate_vec)

def normalize(tokens):
    values = tokens.astype(jnp.float32)
    centre = lax.optimization_barrier(jnp.mean(values, axis=-1, keepdims=True))
    spread = lax.optimization_barrier(jnp.mean((values - centre) ** 2, axis=-1, keepdims=True))
    inv_std = lax.rsqrt(spread + LAYER_EPS)
    return ((values - centre) * inv_std, inv_std)

def norm_backward(out_grad, d_hidden, normed, inv_std, scale_part):
    d_normed = d_hidden * (1.0 + scale_part)
    inner_mean = lax.optimization_barrier(jnp.mean(d_normed, axis=-1, keepdims=True))
    cross_mean = lax.optimization_barrier(jnp.mean(d_normed * normed, axis=-1, keepdims=True))
    d_tokens = out_grad.astype(jnp.float32) + inv_std * (d_normed - inner_mean - normed * cross_mean)
    return d_tokens.astype(jnp.bfloat16)

def group_sum(left_side, right_side, groups):
    left_part = left_side.astype(jnp.float32).reshape(groups, -1, left_side.shape[1])
    right_part = right_side.astype(jnp.float32).reshape(groups, -1, right_side.shape[1])
    partial_sums = jnp.einsum('grd,grf->gdf', left_part, right_part).astype(jnp.bfloat16)
    partial_sums = lax.optimization_barrier(partial_sums)
    return lax.optimization_barrier(jnp.sum(partial_sums.astype(jnp.float32), axis=0)).astype(jnp.bfloat16)

def reference(tokens, out_grad, steps_ids, ada_weight, router_weight, w_in, w_out, chosen):
    images, seq_total, model_width = tokens.shape
    experts = router_weight.shape[1]
    shift_part, scale_part, gate_vec = modulation_parts(steps_ids, ada_weight, model_width)
    normed, inv_std = normalize(tokens)
    hidden = (normed * (1.0 + scale_part) + shift_part).astype(jnp.bfloat16)
    logits = jnp.dot(hidden.reshape(-1, model_width), router_weight, preferred_element_type=jnp.float32)
    router_prob = jax.nn.sigmoid(logits).reshape(images, seq_total, experts)
    image_rows = jnp.arange(images, dtype=jnp.int32)[:, None]

    def expert_step(running, pieces):
        grad_acc, dprob_acc, gate_acc = running
        expert_index, first_weight, second_weight, picks = pieces
        picked_rows = hidden[image_rows, picks]
        picked_grad = out_grad[image_rows, picks].astype(jnp.float32)
        weight = router_prob[image_rows, picks, expert_index]
        flat_rows = picked_rows.reshape(-1, model_width)
        preact = jnp.dot(flat_rows, first_weight, preferred_element_type=jnp.float32)
        gelu_value, gelu_slope = gelu_pair(preact)
        activation = gelu_value.astype(jnp.bfloat16)
        output = jnp.dot(activation, second_weight, preferred_element_type=jnp.float32).astype(jnp.bfloat16)
        output = output.reshape(picked_rows.shape).astype(jnp.float32)
        scaled = gate_vec * picked_grad
        d_output = (weight[..., None] * scaled).astype(jnp.bfloat16).reshape(-1, model_width)
        d_weight = lax.optimization_barrier(jnp.sum(scaled * output, axis=-1))
        gate_acc = gate_acc + lax.optimization_barrier(jnp.sum(weight[..., None] * picked_grad * output, axis=1))
        d_act = jnp.dot(d_output, second_weight.T, preferred_element_type=jnp.float32)
        d_preact = (d_act * gelu_slope).astype(jnp.bfloat16)
        d_rows = jnp.dot(d_preact, first_weight.T, preferred_element_type=jnp.float32).astype(jnp.bfloat16)
        grad_acc = grad_acc.at[image_rows, picks].add(d_rows.reshape(picked_rows.shape).astype(jnp.float32))
        dprob_acc = dprob_acc.at[image_rows, picks, expert_index].set(d_weight)
        first_grad = group_sum(flat_rows, d_preact, N_DP)
        second_grad = group_sum(activation, d_output, N_DP)
        return ((grad_acc, dprob_acc, gate_acc), (first_grad, second_grad))
    start = (jnp.zeros((images, seq_total, model_width), jnp.float32), jnp.zeros((images, seq_total, experts), jnp.float32), jnp.zeros((images, model_width), jnp.float32))
    (grad_acc, dprob_acc, gate_acc), (dw_in, dw_out) = lax.scan(expert_step, start, (jnp.arange(experts, dtype=jnp.int32), w_in, w_out, chosen))
    d_logit = (dprob_acc * router_prob * (1.0 - router_prob)).astype(jnp.bfloat16)
    router_term = jnp.dot(d_logit.reshape(-1, experts), router_weight.T, preferred_element_type=jnp.float32)
    d_hidden = grad_acc + router_term.reshape(images, seq_total, model_width)
    d_shift = lax.optimization_barrier(jnp.sum(d_hidden, axis=1))
    d_scale = lax.optimization_barrier(jnp.sum(d_hidden * normed, axis=1))
    d_modulation = jnp.concatenate([d_shift, d_scale, gate_acc], axis=1)
    d_tokens = norm_backward(out_grad, d_hidden, normed, inv_std, scale_part)
    return (d_tokens, d_modulation, dw_in, dw_out)
```

```python
import math

import jax
import jax.numpy as jnp
import numpy as np
from jax import lax
from jax.sharding import Mesh, PartitionSpec as P

GELU_K = math.sqrt(2.0 / math.pi)
GELU_C = 0.044715
LAYER_EPS = 1e-06
MOST = 6
CHUNKS = 2
PLANE = ("x", "c")
EXPERT = ("z", "x", "c")


def gelu_pair(preact):
    inner_arg = GELU_K * (preact + GELU_C * preact * preact * preact)
    tangent = jnp.tanh(inner_arg)
    gelu_value = 0.5 * preact * (1.0 + tangent)
    gelu_slope = 0.5 * (1.0 + tangent) + 0.5 * preact * (1.0 - tangent * tangent) * GELU_K * (
        1.0 + 3.0 * GELU_C * preact * preact
    )
    return (gelu_value, gelu_slope)


def time_features(steps_ids, feature_count):
    half_width = feature_count // 2
    frequencies = jnp.exp(
        -math.log(10000.0) * jnp.arange(half_width, dtype=jnp.float32) / half_width
    )
    angles = steps_ids.astype(jnp.float32)[:, None] * frequencies[None, :]
    features = jnp.concatenate([jnp.cos(angles), jnp.sin(angles)], axis=1)
    return jax.nn.silu(features).astype(jnp.bfloat16)


def normalize(tokens):
    values = tokens.astype(jnp.float32)
    centre = jnp.mean(values, axis=-1, keepdims=True)
    spread = jnp.mean((values - centre) ** 2, axis=-1, keepdims=True)
    inv_std = lax.rsqrt(spread + LAYER_EPS)
    return ((values - centre) * inv_std, inv_std)


def dot(left, right, dims=((1,), (0,))):
    return lax.dot_general(left, right, (dims, ((), ())), preferred_element_type=jnp.float32)


def shifted(value, axis, step):
    size = lax.axis_size(axis)
    return lax.ppermute(value, axis, [(i, (i + step) % size) for i in range(size)])


def ring_gather(block, axis):
    size = lax.axis_size(axis)
    blocks = {0: block}
    up = down = block
    for step in range(1, size // 2 + 1):
        up = shifted(up, axis, 1)
        blocks[size - step] = up
        if step < size - step:
            down = shifted(down, axis, -1)
            blocks[step] = down
    return jnp.concatenate([blocks[k] for k in range(size)], axis=0)


def ring_scatter(parts, axis):
    size = lax.axis_size(axis)
    far = size // 2
    up = parts[far].astype(jnp.bfloat16)
    down = None
    for step in range(1, far + 1):
        up = shifted(up, axis, 1).astype(jnp.float32)
        if step < far:
            up = (up + parts[far - step]).astype(jnp.bfloat16)
    for step in range(1, size - far):
        mine = parts[far + step]
        down = mine if down is None else down + mine
        down = shifted(down.astype(jnp.bfloat16), axis, -1).astype(jnp.float32)
    total = parts[0] + up
    return total if down is None else total + down


def swap(blocks, axis):
    size = lax.axis_size(axis)
    me = lax.axis_index(axis)
    got = []
    for step in range(size):
        block = lax.dynamic_index_in_dim(blocks, (me + step) % size, 0, keepdims=False)
        got.append(block if step == 0 else shifted(block, axis, step))
    got = jnp.stack(got)
    return [
        lax.dynamic_index_in_dim(got, (me - source) % size, 0, keepdims=False)
        for source in range(size)
    ]


def sum_over(value, axes):
    for axis in axes:
        terms = [shifted(value, axis, step) for step in range(1, lax.axis_size(axis))]
        value = sum(terms, value)
    return value


def body(tokens, out_grad, steps_ids, ada_weight, router_weight, w_in, w_out, chosen):
    images, local_len, width = tokens.shape
    experts = router_weight.shape[1]
    capacity = chosen.shape[2]
    depth, plane_size = lax.axis_size("z"), lax.axis_size(PLANE)
    groups, group = lax.axis_size("dp"), lax.axis_index("dp")
    me_z, me_plane = lax.axis_index("z"), lax.axis_index(PLANE)
    expert_id = lax.axis_index(EXPERT)
    slots = min(MOST * depth, capacity)
    rows = images * capacity
    held = images * local_len
    cols = [slice(i * (width // CHUNKS), (i + 1) * (width // CHUNKS)) for i in range(CHUNKS)]
    first_rows, second_rows = w_in[0], w_out[0]
    ff_part, ff = second_rows.shape[0], first_rows.shape[1]
    width_part = first_rows.shape[0]

    first_weight = lax.all_gather(first_rows, "dp", axis=0, tiled=True)
    all_steps = lax.all_gather(steps_ids, "dp", axis=0, tiled=True)

    image_index = jnp.arange(images, dtype=jnp.int32)
    source = chosen // local_len
    plane_lists = lax.dynamic_slice_in_dim(chosen, me_z * plane_size, plane_size, 0)
    plane_source = plane_lists // local_len
    in_column = plane_source % plane_size == me_plane
    column_rank = jnp.cumsum(in_column.astype(jnp.int32), axis=2) - 1
    place = (
        (plane_source // plane_size - me_z) % depth * held
        + image_index[None, :, None] * local_len
        + plane_lists % local_len
    )
    slot_hot = in_column[..., None] & (
        column_rank[..., None] == jnp.arange(slots, dtype=jnp.int32)
    )
    slot_place = jnp.sum(jnp.where(slot_hot, place[..., None] + 1, 0), axis=2) - 1
    send_table = (
        slot_place.reshape(-1, 1) == jnp.arange(depth * held, dtype=jnp.int32)
    ).astype(jnp.bfloat16)
    own_source = lax.dynamic_index_in_dim(source, expert_id, 0, keepdims=False) % plane_size
    source_hot = (
        own_source[..., None] == jnp.arange(plane_size, dtype=jnp.int32)
    ).astype(jnp.int32)
    own_rank = jnp.sum((jnp.cumsum(source_hot, axis=1) - 1) * source_hot, axis=2)
    landing = own_source * (images * slots) + image_index[:, None] * slots + own_rank
    pick_table = (
        landing.reshape(-1, 1) == jnp.arange(plane_size * images * slots, dtype=jnp.int32)
    ).astype(jnp.bfloat16)

    def fetch(block):
        column = ring_gather(block, "z")
        packed = dot(send_table, column).astype(jnp.bfloat16)
        packed = packed.reshape(plane_size, images * slots, -1)
        got = lax.all_to_all(packed, PLANE, split_axis=0, concat_axis=0, tiled=True)
        return dot(pick_table, got.reshape(plane_size * images * slots, -1)).astype(jnp.bfloat16)

    modulation = dot(time_features(all_steps, ada_weight.shape[0]), ada_weight)
    own_modulation = lax.dynamic_slice_in_dim(modulation, group * images, images, 0)
    shift_part = own_modulation[:, None, :width]
    scale_part = own_modulation[:, None, width : 2 * width]
    gates = modulation[:, None, 2 * width :]

    flat_grad = out_grad.reshape(held, width)
    picked_grad = [fetch(flat_grad[:, c]) for c in cols]
    all_grad = [lax.all_gather(g, "dp", axis=0, tiled=True) for g in picked_grad]
    scaled = [
        (g.reshape(groups * images, capacity, -1) * gates[:, :, c])
        .astype(jnp.bfloat16)
        .reshape(groups * rows, -1)
        for g, c in zip(all_grad, cols)
    ]
    back = sum(dot(s, second_rows[:, c], ((1,), (1,))) for s, c in zip(scaled, cols))
    back = back.astype(jnp.bfloat16).reshape(groups, rows, ff_part)
    d_hidden_units = jnp.concatenate(swap(back, "dp"), axis=1).astype(jnp.float32)

    normed, inv_std = normalize(tokens)
    flat_normed = normed.reshape(held, width).astype(jnp.bfloat16)
    picked = [fetch(flat_normed[:, c]) for c in cols]
    hidden = [
        (n.reshape(images, capacity, -1) * (1.0 + scale_part[:, :, c]) + shift_part[:, :, c])
        .astype(jnp.bfloat16)
        .reshape(rows, -1)
        for n, c in zip(picked, cols)
    ]
    preact = sum(dot(h, first_weight[c]) for h, c in zip(hidden, cols))
    logits = sum(dot(h, router_weight[c]) for h, c in zip(hidden, cols))
    own_column = jnp.arange(experts, dtype=jnp.int32)[None, :] == expert_id
    prob = jax.nn.sigmoid(jnp.sum(jnp.where(own_column, logits, 0.0), axis=1, keepdims=True))
    gelu_value, gelu_slope = gelu_pair(preact)
    weighted = (prob * gelu_value).astype(jnp.bfloat16)
    d_weight = jnp.sum(gelu_value * d_hidden_units, axis=1, keepdims=True)
    d_preact = (prob * d_hidden_units * gelu_slope).astype(jnp.bfloat16)
    d_logit = (d_weight * prob * (1.0 - prob)).astype(jnp.bfloat16)
    d_logits = jnp.where(own_column, d_logit, 0.0).astype(jnp.bfloat16)
    d_rows = [
        dot(d_preact, first_weight[c], ((1,), (1,)))
        + dot(d_logits, router_weight[c], ((1,), (1,)))
        for c in cols
    ]

    d_hidden = []
    for d_row in d_rows:
        packed = dot(pick_table, d_row.astype(jnp.bfloat16), ((0,), (0,))).astype(jnp.bfloat16)
        packed = packed.reshape(plane_size, images * slots, -1)
        got = lax.all_to_all(packed, PLANE, split_axis=0, concat_axis=0, tiled=True)
        parts = dot(send_table, got.reshape(plane_size * images * slots, -1), ((0,), (0,)))
        parts = parts.reshape(depth, held, -1)
        d_hidden.append(ring_scatter([parts[k] for k in range(depth)], "z"))
    d_hidden = jnp.concatenate(d_hidden, axis=1).reshape(images, local_len, width)
    d_normed = d_hidden * (1.0 + scale_part)
    inner_mean = jnp.mean(d_normed, axis=-1, keepdims=True)
    cross_mean = jnp.mean(d_normed * normed, axis=-1, keepdims=True)
    d_tokens = (
        out_grad.astype(jnp.float32) + inv_std * (d_normed - inner_mean - normed * cross_mean)
    ).astype(jnp.bfloat16)

    all_preact = lax.all_gather(d_preact, "dp", axis=0, tiled=True)
    hidden_parts = jnp.stack(
        [
            jnp.concatenate(hidden, axis=1)[:, d * width_part : (d + 1) * width_part]
            for d in range(groups)
        ]
    )
    all_hidden = jnp.concatenate(swap(hidden_parts, "dp"), axis=0)
    dw_in = dot(all_hidden, all_preact, ((0,), (0,))).astype(jnp.bfloat16)[None]
    weighted_parts = jnp.stack(
        [weighted[:, d * ff_part : (d + 1) * ff_part] for d in range(groups)]
    )
    all_weighted = jnp.concatenate(swap(weighted_parts, "dp"), axis=0)
    dw_out = jnp.concatenate(
        [dot(all_weighted, s, ((0,), (0,))).astype(jnp.bfloat16) for s in scaled], axis=1
    )[None]

    gate_grad = jnp.concatenate(
        [
            jnp.sum(
                (g.astype(jnp.float32) * dot(all_weighted, second_rows[:, c])).reshape(
                    groups, images, capacity, -1
                ),
                axis=2,
            )
            for g, c in zip(all_grad, cols)
        ],
        axis=2,
    )
    gate_grad = sum(swap(gate_grad, "dp"))
    d_shift = jnp.concatenate(
        [jnp.sum(d.reshape(images, capacity, -1), axis=1) for d in d_rows], axis=1
    )
    d_scale = jnp.concatenate(
        [
            jnp.sum((d * n.astype(jnp.float32)).reshape(images, capacity, -1), axis=1)
            for d, n in zip(d_rows, picked)
        ],
        axis=1,
    )
    d_modulation = sum_over(jnp.concatenate([d_shift, d_scale, gate_grad], axis=1), EXPERT)
    return (d_tokens, d_modulation, dw_in, dw_out)


def solution(mesh):
    sources, groups = mesh.devices.shape
    cut = Mesh(
        np.asarray(mesh.devices).reshape(sources // 8, 4, 2, groups), ("z", "x", "c", "dp")
    )
    return jax.shard_map(
        body,
        mesh=cut,
        in_specs=(
            P("dp", EXPERT, None),
            P("dp", EXPERT, None),
            P("dp"),
            P(),
            P(),
            P(EXPERT, "dp", None),
            P(EXPERT, "dp", None),
            P(None, "dp", None),
        ),
        out_specs=(
            P("dp", EXPERT, None),
            P("dp", None),
            P(EXPERT, "dp", None),
            P(EXPERT, "dp", None),
        ),
        check_vma=False,
    )
```

```python
import math

import jax
import jax.numpy as jnp
import numpy as np
from jax import lax
from jax.experimental import pallas as pl
from jax.experimental.pallas import tpu as pltpu
from jax.sharding import Mesh, PartitionSpec as P

GELU_K = math.sqrt(2.0 / math.pi)
GELU_C = 0.044715
LAYER_EPS = 1e-06
MOST = 6
TILE = 512
PICK_TILE = 1280
PLANE = ("x", "c")
EXPERT = ("z", "x", "c")
F32, BF16 = jnp.float32, jnp.bfloat16
ANY = pl.BlockSpec(memory_space=pl.ANY)


def gelu_pair(preact):
    inner_arg = GELU_K * (preact + GELU_C * preact * preact * preact)
    tangent = jnp.tanh(inner_arg)
    gelu_value = 0.5 * preact * (1.0 + tangent)
    gelu_slope = 0.5 * (1.0 + tangent) + 0.5 * preact * (1.0 - tangent * tangent) * GELU_K * (
        1.0 + 3.0 * GELU_C * preact * preact
    )
    return (gelu_value, gelu_slope)


def time_features(steps_ids, feature_count):
    half_width = feature_count // 2
    frequencies = jnp.exp(
        -math.log(10000.0) * jnp.arange(half_width, dtype=jnp.float32) / half_width
    )
    angles = steps_ids.astype(jnp.float32)[:, None] * frequencies[None, :]
    features = jnp.concatenate([jnp.cos(angles), jnp.sin(angles)], axis=1)
    return jax.nn.silu(features).astype(jnp.bfloat16)


def standardize(values):
    centre = jnp.mean(values, axis=-1, keepdims=True)
    spread = jnp.mean((values - centre) ** 2, axis=-1, keepdims=True)
    inv_std = lax.rsqrt(spread + LAYER_EPS)
    return ((values - centre) * inv_std, inv_std)


def dot(left, right, dims=((1,), (0,))):
    return lax.dot_general(left, right, (dims, ((), ())), preferred_element_type=F32)


def shape(dims, dtype):
    return jax.ShapeDtypeStruct(dims, dtype)


def whole(*dims):
    return pl.BlockSpec(dims, lambda i: (0,) * len(dims))


def across(rows, tile):
    return pl.BlockSpec((rows, tile), lambda i: (0, i))


def along(tile, cols):
    return pl.BlockSpec((tile, cols), lambda i: (i, 0))


def call(kernel, steps, in_specs, out_specs, out_shape, flops, bytes_accessed, scratch=()):
    return pl.pallas_call(
        kernel,
        grid=(steps,),
        in_specs=in_specs,
        out_specs=out_specs,
        out_shape=out_shape,
        scratch_shapes=scratch,
        compiler_params=pltpu.CompilerParams(
            dimension_semantics=("arbitrary",), vmem_limit_bytes=56 * 1024 * 1024
        ),
        cost_estimate=pl.CostEstimate(
            flops=flops, bytes_accessed=bytes_accessed, transcendentals=0
        ),
    )


def hot(index, rows, cols, along_rows):
    return jnp.where(
        index == lax.broadcasted_iota(jnp.int32, (rows, cols), along_rows), 1.0, 0.0
    ).astype(BF16)


def norm_kernel(tokens_ref, *refs):
    out_ref = refs[-1]
    out_ref[...] = standardize(tokens_ref[...].astype(F32))[0].astype(BF16)


def norm(tokens, after=()):
    rows, width = tokens.shape
    return call(
        norm_kernel, 1, [whole(rows, width)] + [ANY] * len(after), whole(rows, width),
        shape((rows, width), BF16), 10 * rows * width, 4 * rows * width,
    )(tokens, *after)


def pick_kernel(place_ref, column_ref, *refs):
    out_ref = refs[-1]
    column = column_ref[...].reshape(-1, out_ref.shape[1])
    table = hot(place_ref[...], out_ref.shape[0], column.shape[0], 1)
    out_ref[...] = dot(table, column).astype(BF16)


def pick(place, column, image, after=()):
    count, (depth, _, local_len, width) = place.shape[0], column.shape
    tile, held = min(PICK_TILE, width), depth * local_len
    return call(
        pick_kernel, width // tile,
        [whole(count, 1),
         pl.BlockSpec((depth, 1, local_len, tile), lambda i: (0, image, 0, i))]
        + [ANY] * len(after),
        across(count, tile), shape((count, width), BF16), 2 * count * held * width,
        2 * width * (held + count),
    )(place, column, *after)


def join_kernel(group_ref, *refs):
    halves, out_ref = refs[:-1], refs[-1]
    for i, half in enumerate(halves):

        @pl.when(pl.program_id(0) == i)
        def _():
            out_ref[...] = half[...]


def join(halves, group, size):
    rows, width = halves[0].shape
    return pl.pallas_call(
        join_kernel,
        grid_spec=pltpu.PrefetchScalarGridSpec(
            num_scalar_prefetch=1,
            grid=(len(halves),),
            in_specs=[pl.BlockSpec((rows, width), lambda i, g: (0, 0))] * len(halves),
            out_specs=pl.BlockSpec(
                (rows, width), lambda i, g: (lax.rem(g[0] + i // 2, size) * 2 + lax.rem(i, 2), 0)
            ),
        ),
        out_shape=shape((rows * len(halves), width), BF16),
        compiler_params=pltpu.CompilerParams(
            dimension_semantics=("arbitrary",), vmem_limit_bytes=56 * 1024 * 1024
        ),
        cost_estimate=pl.CostEstimate(
            flops=0, bytes_accessed=4 * rows * len(halves) * width, transcendentals=0
        ),
    )(group.reshape(1), *halves)


def picked_rows(landing_ref, got_refs):
    rows = landing_ref.shape[0] // len(got_refs)
    return [
        dot(hot(landing_ref[b * rows : (b + 1) * rows], rows, got.shape[0], 1), got[...])
        for b, got in enumerate(got_refs)
    ]


def grad_kernel(landing_ref, got0_ref, got1_ref, gate_ref, after_ref, pg_ref, scaled_ref):
    picked = picked_rows(landing_ref, (got0_ref, got1_ref))
    pg_ref[...] = jnp.concatenate(picked, axis=0).astype(BF16)
    scaled_ref[...] = jnp.concatenate(
        [p * gate_ref[b : b + 1, :] for b, p in enumerate(picked)], axis=0
    ).astype(BF16)


def grad_rows(landing, got0, got1, gate, after):
    rows, (count, width) = landing.shape[0], got0.shape
    tile = min(PICK_TILE, width)
    return call(
        grad_kernel, width // tile,
        [whole(rows, 1), across(count, tile), across(count, tile), across(gate.shape[0], tile),
         ANY],
        [across(rows, tile), across(rows, tile)],
        [shape((rows, width), BF16), shape((rows, width), BF16)],
        2 * rows * width * count, 4 * width * (count + rows),
    )(landing, got0, got1, gate, after)


def expert_kernel(landing_ref, got0_ref, got1_ref, scale_ref, shift_ref, w_ref, router_ref, u_ref,
                  normed_ref, hidden_ref, d_preact_ref, weighted_ref, d_logit_ref, acc_ref, logit_ref):
    picked = picked_rows(landing_ref, (got0_ref, got1_ref))
    normed_ref[...] = jnp.concatenate(picked, axis=0).astype(BF16)
    hidden = jnp.concatenate(
        [
            p * (1.0 + scale_ref[b : b + 1, :]) + shift_ref[b : b + 1, :]
            for b, p in enumerate(picked)
        ],
        axis=0,
    ).astype(BF16)
    hidden_ref[...] = hidden
    term = dot(hidden, w_ref[...])
    logit = jnp.sum(hidden.astype(F32) * router_ref[...], axis=1, keepdims=True)

    @pl.when(pl.program_id(0) == 0)
    def _():
        acc_ref[...] = term
        logit_ref[...] = logit

    @pl.when(pl.program_id(0) > 0)
    def _():
        acc_ref[...] += term
        logit_ref[...] += logit

    @pl.when(pl.program_id(0) == pl.num_programs(0) - 1)
    def _():
        prob = jax.nn.sigmoid(logit_ref[...])
        gelu_value, gelu_slope = gelu_pair(acc_ref[...])
        u = u_ref[...]
        weighted_ref[...] = (prob * gelu_value).astype(BF16)
        d_preact_ref[...] = (prob * u * gelu_slope).astype(BF16)
        d_weight = jnp.sum(gelu_value * u, axis=1, keepdims=True)
        d_logit_ref[...] = (d_weight * prob * (1.0 - prob)).astype(BF16).astype(F32)


def expert(landing, near, far, scale, shift, first_weight, router, u):
    rows, (count, width) = landing.shape[0], near.shape
    images, ff, tile = scale.shape[0], first_weight.shape[1], min(TILE, near.shape[1])
    return call(
        expert_kernel, width // tile,
        [whole(rows, 1), across(count, tile), across(count, tile), across(images, tile),
         across(images, tile), along(tile, ff), across(1, tile), whole(rows, ff)],
        [across(rows, tile), across(rows, tile), whole(rows, ff), whole(rows, ff), whole(rows, 1)],
        [shape((rows, width), BF16), shape((rows, width), BF16), shape((rows, ff), BF16),
         shape((rows, ff), BF16), shape((rows, 1), F32)],
        2 * rows * width * (ff + 2 * count), 2 * width * (ff + 2 * count + 2 * rows),
        [pltpu.VMEM((rows, ff), F32), pltpu.VMEM((rows, 1), F32)],
    )(landing, near, far, scale, shift, first_weight, router, u)


def rows_kernel(landing_ref, d_preact_ref, w_ref, d_logit_ref, router_ref, normed_ref,
                back0_ref, back1_ref, sums_ref):
    d_rows = dot(d_preact_ref[...], w_ref[...], ((1,), (1,)))
    d_rows += d_logit_ref[...] * router_ref[...]
    half = d_rows.shape[0] // 2
    for b, back_ref in enumerate((back0_ref, back1_ref)):
        mine = slice(b * half, (b + 1) * half)
        table = hot(landing_ref[:, mine], back_ref.shape[0], half, 0)
        back_ref[...] = dot(table, d_rows[mine].astype(BF16)).astype(BF16)
    scaled = d_rows * normed_ref[...].astype(F32)
    sums_ref[...] = jnp.concatenate(
        [jnp.sum(v[b * half : (b + 1) * half], axis=0, keepdims=True)
         for v in (d_rows, scaled) for b in range(2)],
        axis=0,
    )


def row_grads(landing, d_preact, first_weight, d_logit, router, normed, count, count1):
    rows, width = normed.shape
    ff, tile = d_preact.shape[1], min(TILE, width)
    return call(
        rows_kernel, width // tile,
        [whole(1, rows), whole(rows, ff), along(tile, ff), whole(rows, 1), across(1, tile),
         across(rows, tile)],
        [across(count, tile), across(count1, tile), across(4, tile)],
        [shape((count, width), BF16), shape((count1, width), BF16), shape((4, width), F32)],
        2 * rows * width * (ff + 2 * count), 2 * width * (ff + 2 * count + rows),
    )(landing, d_preact, first_weight, d_logit, router, normed)


def spread_kernel(place_ref, got_ref, *refs):
    out_ref = refs[-1]
    table = hot(place_ref[...], out_ref.shape[0], got_ref.shape[0], 0)
    out_ref[...] = dot(table, got_ref[...]).astype(BF16)


def spread(place, got, held, after=()):
    count, width = got.shape
    tile = min(PICK_TILE, width)
    return call(
        spread_kernel, width // tile, [whole(1, count), across(count, tile)] + [ANY] * len(after),
        across(held, tile), shape((held, width), BF16),
        2 * count * held * width, 2 * width * (held + count),
    )(place, got, *after)


def gate_kernel(weighted_ref, w_ref, grad_ref, after_ref, out_ref):
    product = dot(weighted_ref[...], w_ref[...]) * grad_ref[...].astype(F32)
    half = product.shape[0] // 2
    out_ref[...] = jnp.concatenate(
        [jnp.sum(product[b * half : (b + 1) * half], axis=0, keepdims=True) for b in range(2)],
        axis=0,
    )


def gate_sums(weighted, second_weight, grad, after):
    rows, width = grad.shape
    ff, tile = weighted.shape[1], min(TILE, width)
    return call(
        gate_kernel, width // tile,
        [whole(rows, ff), across(ff, tile), across(rows, tile), ANY], across(2, tile),
        shape((2, width), F32), 2 * rows * width * ff, 2 * width * (ff + rows),
    )(weighted, second_weight, grad, after)


def cut_kernel(value_ref, after_ref, out_ref):
    parts, _, part = out_ref.shape
    for d in range(parts):
        out_ref[d] = value_ref[:, d * part : (d + 1) * part]


def cut(value, parts, after):
    rows, width = value.shape
    return call(
        cut_kernel, 1, [whole(rows, width), ANY], whole(parts, rows, width // parts),
        shape((parts, rows, width // parts), BF16), 0, 4 * rows * width,
    )(value, after)


def end_kernel(tokens_ref, grad_ref, *refs):
    out_ref, scale_ref, sum_refs = refs[-1], refs[-2], refs[:-2]
    image = pl.program_id(0)
    normed, inv_std = standardize(tokens_ref[0].astype(F32))
    for b, terms in ((0, sum_refs[:1]), (1, sum_refs[1:])):

        @pl.when(image == b)
        def _():
            d_normed = sum(t[...].astype(F32) for t in terms) * (1.0 + scale_ref[b : b + 1, :])
            inner_mean = jnp.mean(d_normed, axis=-1, keepdims=True)
            cross_mean = jnp.mean(d_normed * normed, axis=-1, keepdims=True)
            out_ref[0] = (
                grad_ref[0].astype(F32)
                + inv_std * (d_normed - inner_mean - normed * cross_mean)
            ).astype(BF16)


def end(tokens, grad, sums, scale):
    images, local_len, width = tokens.shape
    block = pl.BlockSpec((1, local_len, width), lambda i: (i, 0, 0))
    return call(
        end_kernel, images,
        [block] * 2 + [whole(local_len, width)] * len(sums) + [whole(images, width)], block,
        shape(tokens.shape, BF16), 20 * tokens.size, 10 * tokens.size,
    )(tokens, grad, *sums, scale)


def shifted(value, axis, step):
    size = lax.axis_size(axis)
    return lax.ppermute(value, axis, [(i, (i + step) % size) for i in range(size)])


def gather_rows(block, axis):
    size, me = lax.axis_size(axis), lax.axis_index(axis)
    rows = block.shape[0] // 2
    own = [block[:rows], block[rows:]]
    if size == 1:
        return block, own, own
    below = [shifted(h, axis, 1) for h in own]
    above = [shifted(h, axis, -1) for h in own]
    if size == 2:
        return join(own + above, me, size), below, above
    far = [shifted(below[0], axis, 1), shifted(above[1], axis, -1)]
    return join(own + above + far + below, me, size), below + above, far


def swap(blocks, axis):
    size = lax.axis_size(axis)
    me = lax.axis_index(axis)
    got = []
    for step in range(size):
        block = lax.dynamic_index_in_dim(blocks, (me + step) % size, 0, keepdims=False)
        got.append(block if step == 0 else shifted(block, axis, step))
    got = jnp.stack(got)
    return [
        lax.dynamic_index_in_dim(got, (me - source) % size, 0, keepdims=False)
        for source in range(size)
    ]


def sum_over(value, axes):
    for axis in axes:
        step = 1
        while step < lax.axis_size(axis):
            value = value + shifted(value, axis, step)
            step *= 2
    return value


def body(tokens, out_grad, steps_ids, ada_weight, router_weight, w_in, w_out, chosen):
    images, local_len, width = tokens.shape
    capacity = chosen.shape[2]
    depth, plane_size = lax.axis_size("z"), lax.axis_size(PLANE)
    groups = lax.axis_size("dp")
    me_z, me_plane = lax.axis_index("z"), lax.axis_index(PLANE)
    expert_id = lax.axis_index(EXPERT)
    rows, held = images * capacity, images * local_len
    slots = min(MOST * depth, capacity)
    count = plane_size * slots

    second_weight, second_near, second_far = gather_rows(w_out[0], "dp")
    first_weight, first_near, first_far = gather_rows(w_in[0], "dp")

    plane_lists = lax.dynamic_slice_in_dim(chosen, me_z * plane_size, plane_size, 0)
    block = plane_lists // local_len
    mine = block % plane_size == me_plane
    place = block // plane_size * local_len + plane_lists % local_len
    rank = jnp.cumsum(mine.astype(jnp.int32), axis=2) - 1
    slot_hot = mine[..., None] & (rank[..., None] == jnp.arange(slots, dtype=jnp.int32))
    places = jnp.sum(jnp.where(slot_hot, place[..., None] + 1, 0), axis=2) - 1
    places = [places[:, b].reshape(count) for b in range(images)]
    own_list = lax.dynamic_index_in_dim(chosen, expert_id, 0, keepdims=False)
    column = own_list // local_len % plane_size
    column_hot = (
        column[..., None] == jnp.arange(plane_size, dtype=jnp.int32)
    ).astype(jnp.int32)
    rank = jnp.sum((jnp.cumsum(column_hot, axis=1) - 1) * column_hot, axis=2)
    landing = (column * slots + rank).reshape(rows)

    modulation = dot(time_features(steps_ids, ada_weight.shape[0]), ada_weight)
    shift, scale, gate = (modulation[:, i * width : (i + 1) * width] for i in range(3))
    router = lax.dynamic_slice_in_dim(router_weight, expert_id, 1, 1).astype(F32).reshape(1, width)

    def exchange(packed):
        packed = packed.reshape(plane_size, slots, width)
        got = lax.all_to_all(packed, PLANE, split_axis=0, concat_axis=0, tiled=True)
        return got.reshape(count, width)

    def column_of(value):
        return lax.all_gather(value, "z", axis=0, tiled=False)

    def pack(b, column, image, after):
        return pick(places[b][:, None], column, image, after)

    grad_column = column_of(out_grad)
    normed_column0 = column_of(norm(tokens[0])[None])
    normed_column1 = column_of(norm(tokens[1], second_near + [first_near[0], first_near[-1]])[None])
    packed_grad0 = pack(0, grad_column, 0, [])
    packed_grad1 = pack(1, grad_column, 1, second_far + first_near[1:-1])
    got_grad0, got_grad1 = exchange(packed_grad0), exchange(packed_grad1)
    packed_normed0 = pack(0, normed_column0, 0, first_far + [got_grad0])
    got_normed0 = exchange(packed_normed0)
    picked_grad, scaled = grad_rows(
        landing[:, None], got_grad0, got_grad1, gate, packed_normed0
    )
    all_scaled = lax.all_gather(scaled, "dp", axis=0, tiled=True)
    u = dot(scaled, second_weight, ((1,), (1,)))
    packed_normed1 = pack(1, normed_column1, 0, [first_weight, scaled, u, got_normed0])
    got_normed1 = exchange(packed_normed1)
    normed, hidden, d_preact, weighted, d_logit = expert(
        landing[:, None], got_normed0, got_normed1, scale, shift, first_weight, router, u
    )
    *back, sums = row_grads(
        landing[None, :], d_preact, first_weight, d_logit, router, normed, count, count
    )
    all_preact = lax.all_gather(d_preact, "dp", axis=0, tiled=True)

    part0 = spread(places[0][None, :], exchange(back[0]), depth * local_len, [all_scaled])
    part1 = spread(places[1][None, :], exchange(back[1]), depth * local_len)
    sums_back = [
        lax.psum_scatter(p, "z", scatter_dimension=0, tiled=True) for p in (part0, part1)
    ]
    d_tokens = end(tokens, out_grad, sums_back, scale)

    all_hidden = jnp.concatenate(swap(cut(hidden, groups, part0), "dp"), axis=0)
    dw_in = dot(all_hidden, all_preact, ((0,), (0,))).astype(BF16)[None]
    all_weighted = jnp.concatenate(swap(cut(weighted, groups, part0), "dp"), axis=0)
    dw_out = dot(all_weighted, all_scaled, ((0,), (0,))).astype(BF16)[None]

    gate_grad = gate_sums(weighted, second_weight, picked_grad, part0)
    d_modulation = sum_over(
        jnp.concatenate([sums[:images], sums[images:], gate_grad], axis=1), EXPERT
    )
    return (d_tokens, d_modulation, dw_in, dw_out)


def solution(mesh):
    sources, groups = mesh.devices.shape
    fine = Mesh(
        np.asarray(mesh.devices).reshape(sources // 8, 4, 2, groups), ("z", "x", "c", "dp")
    )
    return jax.shard_map(
        body,
        mesh=fine,
        in_specs=(
            P("dp", EXPERT, None),
            P("dp", EXPERT, None),
            P("dp"),
            P(),
            P(),
            P(EXPERT, "dp", None),
            P(EXPERT, "dp", None),
            P(None, "dp", None),
        ),
        out_specs=(
            P("dp", EXPERT, None),
            P("dp", None),
            P(EXPERT, "dp", None),
            P(EXPERT, "dp", None),
        ),
        check_vma=False,
    )
```

```python
import functools
import math

import jax
import jax.numpy as jnp
import numpy as np
from jax import lax
from jax.experimental import pallas as pl
from jax.experimental.pallas import tpu as pltpu
from jax.sharding import Mesh, PartitionSpec as P

GELU_K = math.sqrt(2.0 / math.pi)
GELU_C = 0.044715
LAYER_EPS = 1e-06
MOST = 6
TILE = 512
PICK_TILE = 1280
OUTER_TILE = 640
PLANE = ("x", "c")
EXPERT = ("z", "x", "c")
F32, BF16 = jnp.float32, jnp.bfloat16
ANY = pl.BlockSpec(memory_space=pl.ANY)


def gelu_pair(preact):
    inner_arg = GELU_K * (preact + GELU_C * preact * preact * preact)
    tangent = jnp.tanh(inner_arg)
    gelu_value = 0.5 * preact * (1.0 + tangent)
    gelu_slope = 0.5 * (1.0 + tangent) + 0.5 * preact * (1.0 - tangent * tangent) * GELU_K * (
        1.0 + 3.0 * GELU_C * preact * preact
    )
    return (gelu_value, gelu_slope)


def time_features(steps_ids, feature_count):
    half_width = feature_count // 2
    frequencies = jnp.exp(
        -math.log(10000.0) * jnp.arange(half_width, dtype=jnp.float32) / half_width
    )
    angles = steps_ids.astype(jnp.float32)[:, None] * frequencies[None, :]
    features = jnp.concatenate([jnp.cos(angles), jnp.sin(angles)], axis=1)
    return jax.nn.silu(features).astype(jnp.bfloat16)


def standardize(values):
    centre = jnp.mean(values, axis=-1, keepdims=True)
    spread = jnp.mean((values - centre) ** 2, axis=-1, keepdims=True)
    inv_std = lax.rsqrt(spread + LAYER_EPS)
    return ((values - centre) * inv_std, inv_std)


def dot(left, right, dims=((1,), (0,))):
    return lax.dot_general(left, right, (dims, ((), ())), preferred_element_type=F32)


def shape(dims, dtype):
    return jax.ShapeDtypeStruct(dims, dtype)


def whole(*dims):
    return pl.BlockSpec(dims, lambda i: (0,) * len(dims))


def across(rows, tile):
    return pl.BlockSpec((rows, tile), lambda i: (0, i))


def along(tile, cols):
    return pl.BlockSpec((tile, cols), lambda i: (i, 0))


def call(kernel, steps, in_specs, out_specs, out_shape, flops, bytes_accessed, scratch=()):
    return pl.pallas_call(
        kernel,
        grid=(steps,),
        in_specs=in_specs,
        out_specs=out_specs,
        out_shape=out_shape,
        scratch_shapes=scratch,
        compiler_params=pltpu.CompilerParams(
            dimension_semantics=("arbitrary",), vmem_limit_bytes=56 * 1024 * 1024
        ),
        cost_estimate=pl.CostEstimate(
            flops=flops, bytes_accessed=bytes_accessed, transcendentals=0
        ),
    )


def hot(index, rows, cols, along_rows):
    return jnp.where(
        index == lax.broadcasted_iota(jnp.int32, (rows, cols), along_rows), 1.0, 0.0
    ).astype(BF16)


def norm_kernel(tokens_ref, *refs):
    out_ref = refs[-1]
    out_ref[...] = standardize(tokens_ref[...].astype(F32))[0].astype(BF16)


def norm(tokens, after=()):
    rows, width = tokens.shape
    return call(
        norm_kernel, 1, [whole(rows, width)] + [ANY] * len(after), whole(rows, width),
        shape((rows, width), BF16), 10 * rows * width, 4 * rows * width,
    )(tokens, *after)


def pick_kernel(place_ref, column_ref, *refs):
    out_ref = refs[-1]
    column = column_ref[...].reshape(-1, out_ref.shape[1])
    table = hot(place_ref[...], out_ref.shape[0], column.shape[0], 1)
    out_ref[...] = dot(table, column).astype(BF16)


def pick(place, column, image, after=()):
    count, (depth, _, local_len, width) = place.shape[0], column.shape
    tile, held = min(PICK_TILE, width), depth * local_len
    return call(
        pick_kernel, width // tile,
        [whole(count, 1),
         pl.BlockSpec((depth, 1, local_len, tile), lambda i: (0, image, 0, i))]
        + [ANY] * len(after),
        across(count, tile), shape((count, width), BF16), 2 * count * held * width,
        2 * width * (held + count),
    )(place, column, *after)


def join_kernel(group_ref, *refs):
    halves, out_ref = refs[:-1], refs[-1]
    for i, half in enumerate(halves):

        @pl.when(pl.program_id(0) == i)
        def _():
            out_ref[...] = half[...]


def join(halves, group, size):
    rows, width = halves[0].shape
    return pl.pallas_call(
        join_kernel,
        grid_spec=pltpu.PrefetchScalarGridSpec(
            num_scalar_prefetch=1,
            grid=(len(halves),),
            in_specs=[pl.BlockSpec((rows, width), lambda i, g: (0, 0))] * len(halves),
            out_specs=pl.BlockSpec(
                (rows, width), lambda i, g: (lax.rem(g[0] + i // 2, size) * 2 + lax.rem(i, 2), 0)
            ),
        ),
        out_shape=shape((rows * len(halves), width), BF16),
        compiler_params=pltpu.CompilerParams(
            dimension_semantics=("arbitrary",), vmem_limit_bytes=56 * 1024 * 1024
        ),
        cost_estimate=pl.CostEstimate(
            flops=0, bytes_accessed=4 * rows * len(halves) * width, transcendentals=0
        ),
    )(group.reshape(1), *halves)


def picked_rows(landing_ref, got_refs):
    rows = landing_ref.shape[0] // len(got_refs)
    return [
        dot(hot(landing_ref[b * rows : (b + 1) * rows], rows, got.shape[0], 1), got[...])
        for b, got in enumerate(got_refs)
    ]


def grad_kernel(landing_ref, got0_ref, got1_ref, gate_ref, after_ref, pg_ref, scaled_ref):
    picked = picked_rows(landing_ref, (got0_ref, got1_ref))
    pg_ref[...] = jnp.concatenate(picked, axis=0).astype(BF16)
    scaled_ref[...] = jnp.concatenate(
        [p * gate_ref[b : b + 1, :] for b, p in enumerate(picked)], axis=0
    ).astype(BF16)


def grad_rows(landing, got0, got1, gate, after):
    rows, (count, width) = landing.shape[0], got0.shape
    tile = min(PICK_TILE, width)
    return call(
        grad_kernel, width // tile,
        [whole(rows, 1), across(count, tile), across(count, tile), across(gate.shape[0], tile),
         ANY],
        [across(rows, tile), across(rows, tile)],
        [shape((rows, width), BF16), shape((rows, width), BF16)],
        2 * rows * width * count, 4 * width * (count + rows),
    )(landing, got0, got1, gate, after)


def expert_kernel(landing_ref, got_ref, scale_ref, shift_ref, w_ref, router_ref, u_ref, after_ref,
                  normed_ref, hidden_ref, d_preact_ref, weighted_ref, d_logit_ref, acc_ref, logit_ref):
    picked = dot(hot(landing_ref[...], landing_ref.shape[0], got_ref.shape[0], 1), got_ref[...])
    normed_ref[...] = picked.astype(BF16)
    hidden = (picked * (1.0 + scale_ref[...]) + shift_ref[...]).astype(BF16)
    hidden_ref[...] = hidden
    term = dot(hidden, w_ref[...])
    logit = jnp.sum(hidden.astype(F32) * router_ref[...], axis=1, keepdims=True)

    @pl.when(pl.program_id(0) == 0)
    def _():
        acc_ref[...] = term
        logit_ref[...] = logit

    @pl.when(pl.program_id(0) > 0)
    def _():
        acc_ref[...] += term
        logit_ref[...] += logit

    @pl.when(pl.program_id(0) == pl.num_programs(0) - 1)
    def _():
        prob = jax.nn.sigmoid(logit_ref[...])
        gelu_value, gelu_slope = gelu_pair(acc_ref[...])
        u = u_ref[...]
        weighted_ref[...] = (prob * gelu_value).astype(BF16)
        d_preact_ref[...] = (prob * u * gelu_slope).astype(BF16)
        d_weight = jnp.sum(gelu_value * u, axis=1, keepdims=True)
        d_logit_ref[...] = (d_weight * prob * (1.0 - prob)).astype(BF16).astype(F32)


def expert(image, landing, got, scale, shift, first_weight, router, u, after):
    rows, (count, width) = landing.shape[0], got.shape
    ff, tile = first_weight.shape[1], min(TILE, width)
    return call(
        expert_kernel, width // tile,
        [whole(rows, 1), across(count, tile), across(1, tile), across(1, tile), along(tile, ff),
         across(1, tile), pl.BlockSpec((rows, ff), lambda i: (image, 0)), ANY],
        [across(rows, tile), across(rows, tile), whole(rows, ff), whole(rows, ff), whole(rows, 1)],
        [shape((rows, width), BF16), shape((rows, width), BF16), shape((rows, ff), BF16),
         shape((rows, ff), BF16), shape((rows, 1), F32)],
        2 * rows * width * (ff + count), 2 * width * (ff + count + 2 * rows),
        [pltpu.VMEM((rows, ff), F32), pltpu.VMEM((rows, 1), F32)],
    )(landing, got, scale, shift, first_weight, router, u, after)


def rows_kernel(landing_ref, d_preact_ref, w_ref, d_logit_ref, router_ref, normed_ref, *refs):
    back_ref, sums_ref = refs[-2:]
    d_rows = dot(d_preact_ref[...], w_ref[...], ((1,), (1,)))
    d_rows += d_logit_ref[...] * router_ref[...]
    table = hot(landing_ref[...], back_ref.shape[0], d_rows.shape[0], 0)
    back_ref[...] = dot(table, d_rows.astype(BF16)).astype(BF16)
    scaled = d_rows * normed_ref[...].astype(F32)
    sums_ref[...] = jnp.concatenate(
        [jnp.sum(v, axis=0, keepdims=True) for v in (d_rows, scaled)], axis=0
    )


def row_grads(landing, d_preact, first_weight, d_logit, router, normed, count, after):
    rows, width = normed.shape
    ff, tile = d_preact.shape[1], min(TILE, width)
    return call(
        rows_kernel, width // tile,
        [whole(1, rows), whole(rows, ff), along(tile, ff), whole(rows, 1), across(1, tile),
         across(rows, tile)] + [ANY] * len(after),
        [across(count, tile), across(2, tile)],
        [shape((count, width), BF16), shape((2, width), F32)],
        2 * rows * width * (ff + count), 2 * width * (ff + count + rows),
    )(landing, d_preact, first_weight, d_logit, router, normed, *after)


def spread_kernel(place_ref, got_ref, *refs):
    out_ref = refs[-1]
    table = hot(place_ref[...], out_ref.shape[0], got_ref.shape[0], 0)
    out_ref[...] = dot(table, got_ref[...]).astype(BF16)


def spread(place, got, held, after=()):
    count, width = got.shape
    tile = min(PICK_TILE, width)
    return call(
        spread_kernel, width // tile, [whole(1, count), across(count, tile)] + [ANY] * len(after),
        across(held, tile), shape((held, width), BF16),
        2 * count * held * width, 2 * width * (held + count),
    )(place, got, *after)


def gate_kernel(weighted0_ref, weighted1_ref, w_ref, grad_ref, after_ref, out_ref):
    half = weighted0_ref.shape[0]
    weighted = jnp.concatenate([weighted0_ref[...], weighted1_ref[...]], axis=0)
    product = dot(weighted, w_ref[...]) * grad_ref[...].astype(F32)
    out_ref[...] = jnp.concatenate(
        [jnp.sum(product[b * half : (b + 1) * half], axis=0, keepdims=True) for b in range(2)],
        axis=0,
    )


def gate_sums(weighted, second_weight, grad, after):
    rows, width = grad.shape
    ff, tile = weighted[0].shape[1], min(PICK_TILE, width)
    return call(
        gate_kernel, width // tile,
        [whole(rows // 2, ff)] * 2 + [across(ff, tile), across(rows, tile), ANY], across(2, tile),
        shape((2, width), F32), 2 * rows * width * ff, 2 * width * (ff + rows),
    )(*weighted, second_weight, grad, after)


def cut_kernel(with_pre, pre_ref, hidden_ref, weighted_ref, after_ref, out_ref):
    parts, rows, total = out_ref.shape
    ff = pre_ref.shape[1] if with_pre else 0
    first, second = hidden_ref.shape[1] // parts, weighted_ref.shape[1] // parts
    used = ff + first + second
    for d in range(parts):
        if with_pre:
            out_ref[d, :, :ff] = pre_ref[...]
        out_ref[d, :, ff : ff + first] = hidden_ref[:, d * first : (d + 1) * first]
        out_ref[d, :, ff + first : used] = weighted_ref[:, d * second : (d + 1) * second]
        if used < total:
            out_ref[d, :, used:] = jnp.zeros((rows, total - used), BF16)


def cut(pre, hidden, weighted, with_pre, parts, after):
    (rows, width), ff = hidden.shape, weighted.shape[1]
    part = (ff if with_pre else 0) + (width + ff) // parts
    part += -part % 128
    return call(
        functools.partial(cut_kernel, with_pre), 1,
        [whole(rows, ff), whole(rows, width), whole(rows, ff), ANY],
        whole(parts, rows, part), shape((parts, rows, part), BF16), 0,
        2 * rows * (width + 2 * ff + parts * part),
    )(pre, hidden, weighted, after)


def hold_kernel(value_ref, *refs):
    refs[-1][...] = value_ref[...]


def hold(value, after):
    return call(
        hold_kernel, 1, [whole(*value.shape)] + [ANY] * len(after), whole(*value.shape),
        shape(value.shape, BF16), 0, 4 * value.size,
    )(value, *after)


def outer_kernel(count, left_at, group_ref, *refs):
    left, right, out_ref = refs[: 2 * count], refs[2 * count : -2], refs[-1]
    tall, wide = out_ref.shape
    total = None
    for k in range(count):
        rights = list(right[k * len(right) // count : (k + 1) * len(right) // count])
        rights = [r[...].reshape(-1, wide) for r in rights]
        if len(rights) == 1:
            rights.append(left[2 * k + 1][:, :wide])
        lefts = [left[2 * k + b][:, left_at[b] : left_at[b] + tall] for b in range(2)]
        term = dot(
            jnp.concatenate(lefts, axis=0), jnp.concatenate(rights, axis=0), ((0,), (0,))
        )
        total = term if total is None else total + term
    out_ref[...] = total.astype(BF16)


def outer(sent, left_at, tall, right, group, after):
    (rows, _), count = sent[0].shape, len(sent) // 2
    both = right.shape[1] // rows
    wide = right.shape[2]
    tile = min(OUTER_TILE, wide) if both == 2 else wide
    right_specs = [
        pl.BlockSpec(
            (1, rows, tile), lambda i, g, k=k, b=b: (lax.rem(g[0] + count - k, count), b, i)
        )
        for k in range(count)
        for b in range(both)
    ]
    return pl.pallas_call(
        functools.partial(outer_kernel, count, left_at),
        grid_spec=pltpu.PrefetchScalarGridSpec(
            num_scalar_prefetch=1,
            grid=(wide // tile,),
            in_specs=[pl.BlockSpec(p.shape, lambda i, g: (0, 0)) for p in sent]
            + right_specs + [ANY],
            out_specs=pl.BlockSpec((tall, tile), lambda i, g: (0, i)),
        ),
        out_shape=shape((tall, wide), BF16),
        compiler_params=pltpu.CompilerParams(
            dimension_semantics=("arbitrary",), vmem_limit_bytes=56 * 1024 * 1024
        ),
        cost_estimate=pl.CostEstimate(
            flops=4 * rows * count * tall * wide,
            bytes_accessed=2 * (2 * rows * count * (tall + wide) + tall * wide), transcendentals=0,
        ),
    )(group.reshape(1), *sent, *([right] * len(right_specs)), after)


def end_kernel(tokens_ref, grad_ref, *refs):
    out_ref, scale_ref, sum_refs = refs[-1], refs[-2], refs[:-2]
    image = pl.program_id(0)
    normed, inv_std = standardize(tokens_ref[0].astype(F32))
    for b, terms in ((0, sum_refs[:1]), (1, sum_refs[1:])):

        @pl.when(image == b)
        def _():
            d_normed = sum(t[...].astype(F32) for t in terms) * (1.0 + scale_ref[b : b + 1, :])
            inner_mean = jnp.mean(d_normed, axis=-1, keepdims=True)
            cross_mean = jnp.mean(d_normed * normed, axis=-1, keepdims=True)
            out_ref[0] = (
                grad_ref[0].astype(F32)
                + inv_std * (d_normed - inner_mean - normed * cross_mean)
            ).astype(BF16)


def end(tokens, grad, sums, scale):
    images, local_len, width = tokens.shape
    block = pl.BlockSpec((1, local_len, width), lambda i: (i, 0, 0))
    return call(
        end_kernel, images,
        [block] * 2 + [whole(local_len, width)] * len(sums) + [whole(images, width)], block,
        shape(tokens.shape, BF16), 20 * tokens.size, 10 * tokens.size,
    )(tokens, grad, *sums, scale)


def shifted(value, axis, step):
    size = lax.axis_size(axis)
    return lax.ppermute(value, axis, [(i, (i + step) % size) for i in range(size)])


def gather_rows(block, axis):
    size, me = lax.axis_size(axis), lax.axis_index(axis)
    rows = block.shape[0] // 2
    own = [block[:rows], block[rows:]]
    if size == 1:
        return block, own, own
    below = [shifted(h, axis, 1) for h in own]
    above = [shifted(h, axis, -1) for h in own]
    if size == 2:
        return join(own + above, me, size), below, above
    far = [shifted(below[0], axis, 1), shifted(above[1], axis, -1)]
    return join(own + above + far + below, me, size), below + above, far


def swap(blocks, axis):
    size, me = lax.axis_size(axis), lax.axis_index(axis)
    cut = [
        lax.dynamic_index_in_dim(blocks, (me + step) % size, 0, keepdims=False)
        for step in range(size)
    ]
    return [cut[0]] + [shifted(cut[step], axis, step) for step in range(1, size)]


def sum_over(value, axes):
    size = lax.axis_size(axes)
    parts = value.reshape(size, -1)
    parts = lax.all_to_all(parts, axes, split_axis=0, concat_axis=0, tiled=True)
    total = jnp.broadcast_to(jnp.sum(parts, axis=0, keepdims=True), parts.shape)
    total = lax.all_to_all(total, axes, split_axis=0, concat_axis=0, tiled=True)
    return total.reshape(value.shape)


def body(tokens, out_grad, steps_ids, ada_weight, router_weight, w_in, w_out, chosen):
    images, local_len, width = tokens.shape
    capacity = chosen.shape[2]
    depth, plane_size = lax.axis_size("z"), lax.axis_size(PLANE)
    groups = lax.axis_size("dp")
    me_z, me_plane = lax.axis_index("z"), lax.axis_index(PLANE)
    expert_id = lax.axis_index(EXPERT)
    rows, held = images * capacity, images * local_len
    slots = min(MOST * depth, capacity)
    count = plane_size * slots

    second_weight, second_near, second_far = gather_rows(w_out[0], "dp")
    first_weight, first_near, first_far = gather_rows(w_in[0], "dp")

    plane_lists = lax.dynamic_slice_in_dim(chosen, me_z * plane_size, plane_size, 0)
    block = plane_lists // local_len
    mine = block % plane_size == me_plane
    place = block // plane_size * local_len + plane_lists % local_len
    rank = jnp.cumsum(mine.astype(jnp.int32), axis=2) - 1
    slot_hot = mine[..., None] & (rank[..., None] == jnp.arange(slots, dtype=jnp.int32))
    places = jnp.sum(jnp.where(slot_hot, place[..., None] + 1, 0), axis=2) - 1
    places = [places[:, b].reshape(count) for b in range(images)]
    own_list = lax.dynamic_index_in_dim(chosen, expert_id, 0, keepdims=False)
    column = own_list // local_len % plane_size
    column_hot = (
        column[..., None] == jnp.arange(plane_size, dtype=jnp.int32)
    ).astype(jnp.int32)
    rank = jnp.sum((jnp.cumsum(column_hot, axis=1) - 1) * column_hot, axis=2)
    landing = (column * slots + rank).reshape(rows)

    group = lax.axis_index("dp")
    modulation = dot(time_features(steps_ids, ada_weight.shape[0]), ada_weight)
    shift, scale, gate = (modulation[:, i * width : (i + 1) * width] for i in range(3))
    router = lax.dynamic_slice_in_dim(router_weight, expert_id, 1, 1).astype(F32).reshape(1, width)

    def exchange(packed):
        packed = packed.reshape(plane_size, slots, width)
        got = lax.all_to_all(packed, PLANE, split_axis=0, concat_axis=0, tiled=True)
        return got.reshape(count, width)

    def column_of(value):
        return lax.all_gather(value, "z", axis=0, tiled=False)

    def pack(b, column, image, after):
        return pick(places[b][:, None], column, image, after)

    grad_column = column_of(out_grad)
    normed_column0 = column_of(norm(tokens[0])[None])
    normed_column1 = column_of(norm(tokens[1], second_near + [first_near[0], first_near[-1]])[None])
    packed_grad0 = pack(0, grad_column, 0, [])
    packed_grad1 = pack(1, grad_column, 1, [])
    got_grad0, got_grad1 = exchange(packed_grad0), exchange(packed_grad1)
    packed_normed0 = pack(
        0, normed_column0, 0, second_far + first_near[1:-1] + [got_grad0]
    )
    got_normed0 = exchange(packed_normed0)
    picked_grad, scaled = grad_rows(
        landing[:, None], got_grad0, got_grad1, gate, packed_normed0
    )
    u = dot(scaled, second_weight, ((1,), (1,)))
    packed_normed1 = pack(1, normed_column1, 0, [u, got_normed0] + first_far)
    got_normed1 = exchange(packed_normed1)
    all_scaled = lax.all_gather(scaled, "dp", axis=0, tiled=False)

    hidden, d_preact, weighted, got_back, sums = [], [], [], [], []
    for b, got in enumerate((got_normed0, got_normed1)):
        own = slice(b * capacity, (b + 1) * capacity)
        normed_b, hidden_b, d_preact_b, weighted_b, d_logit_b = expert(
            b, landing[own, None], got, scale[b : b + 1], shift[b : b + 1], first_weight, router,
            u, packed_normed1 if b == 0 else held_preact,
        )
        back_b, sums_b = row_grads(
            landing[None, own], d_preact_b, first_weight, d_logit_b, router, normed_b, count,
            [got_normed1 if b == 0 else got_back[0]],
        )
        if b == 0:
            held_preact = hold(d_preact_b, [all_scaled, back_b])
        for kept, value in zip(
            (hidden, d_preact, weighted, got_back, sums),
            (hidden_b, d_preact_b, weighted_b, exchange(back_b), sums_b),
        ):
            kept.append(value)
    gate_grad = gate_sums(weighted, second_weight, picked_grad, back_b)
    all_preact = lax.all_gather(held_preact, "dp", axis=0, tiled=False)
    sent = [
        swap(cut(d_preact[b], hidden[b], weighted[b], b == 1, groups, after), "dp")
        for b, after in ((0, d_preact[1]), (1, back_b))
    ]
    part0 = spread(
        places[0][None, :], got_back[0], depth * local_len,
        [d_preact[1], sent[0][0]],
    )
    part1 = spread(
        places[1][None, :], got_back[1], depth * local_len,
        [gate_grad, sent[1][0]] + sent[0][1:],
    )
    sums_back = [
        lax.psum_scatter(p, "z", scatter_dimension=0, tiled=True) for p in (part0, part1)
    ]
    d_tokens = end(tokens, out_grad, sums_back, scale)

    d_modulation = sum_over(
        jnp.concatenate(
            [jnp.concatenate([s[i : i + 1] for s in sums], axis=0) for i in range(2)]
            + [gate_grad],
            axis=1,
        ),
        EXPERT,
    )

    pieces = [piece for pair in zip(*sent) for piece in pair]
    ff, first, second = first_weight.shape[1], w_in.shape[1], w_out.shape[1]
    dw_in = outer(pieces, (0, ff), first, all_preact, group, d_modulation)[None]
    dw_out = outer(pieces, (first, ff + first), second, all_scaled, group, d_modulation)[None]
    return (d_tokens, d_modulation, dw_in, dw_out)


def solution(mesh):
    sources, groups = mesh.devices.shape
    fine = Mesh(
        np.asarray(mesh.devices).reshape(sources // 8, 4, 2, groups), ("z", "x", "c", "dp")
    )
    return jax.shard_map(
        body,
        mesh=fine,
        in_specs=(
            P("dp", EXPERT, None),
            P("dp", EXPERT, None),
            P("dp"),
            P(),
            P(),
            P(EXPERT, "dp", None),
            P(EXPERT, "dp", None),
            P(None, "dp", None),
        ),
        out_specs=(
            P("dp", EXPERT, None),
            P("dp", None),
            P(EXPERT, "dp", None),
            P(EXPERT, "dp", None),
        ),
        check_vma=False,
    )
```

```python
import functools
import math

import jax
import jax.numpy as jnp
import numpy as np
from jax import lax
from jax.experimental import pallas as pl
from jax.experimental.pallas import tpu as pltpu
from jax.sharding import Mesh, PartitionSpec as P

GELU_K = math.sqrt(2.0 / math.pi)
GELU_C = 0.044715
LAYER_EPS = 1e-06
MOST = 6
TILE = 1280
PICK_TILE = 1280
OUTER_TILE = 1280
PLANE = ("x", "c")
EXPERT = ("z", "x", "c")
F32, BF16 = jnp.float32, jnp.bfloat16
ANY = pl.BlockSpec(memory_space=pl.ANY)


def gelu_pair(preact):
    inner_arg = GELU_K * (preact + GELU_C * preact * preact * preact)
    tangent = jnp.tanh(inner_arg)
    gelu_value = 0.5 * preact * (1.0 + tangent)
    gelu_slope = 0.5 * (1.0 + tangent) + 0.5 * preact * (1.0 - tangent * tangent) * GELU_K * (
        1.0 + 3.0 * GELU_C * preact * preact
    )
    return (gelu_value, gelu_slope)


def time_features(steps_ids, feature_count):
    half_width = feature_count // 2
    frequencies = jnp.exp(
        -math.log(10000.0) * jnp.arange(half_width, dtype=jnp.float32) / half_width
    )
    angles = steps_ids.astype(jnp.float32)[:, None] * frequencies[None, :]
    features = jnp.concatenate([jnp.cos(angles), jnp.sin(angles)], axis=1)
    return jax.nn.silu(features).astype(jnp.bfloat16)


def standardize(values):
    centre = jnp.mean(values, axis=-1, keepdims=True)
    spread = jnp.mean((values - centre) ** 2, axis=-1, keepdims=True)
    inv_std = lax.rsqrt(spread + LAYER_EPS)
    return ((values - centre) * inv_std, inv_std)


def dot(left, right, dims=((1,), (0,))):
    return lax.dot_general(left, right, (dims, ((), ())), preferred_element_type=F32)


def shape(dims, dtype):
    return jax.ShapeDtypeStruct(dims, dtype)


def whole(*dims):
    return pl.BlockSpec(dims, lambda i: (0,) * len(dims))


def across(rows, tile):
    return pl.BlockSpec((rows, tile), lambda i: (0, i))


def along(tile, cols):
    return pl.BlockSpec((tile, cols), lambda i: (i, 0))


def call(kernel, steps, in_specs, out_specs, out_shape, flops, bytes_accessed, scratch=()):
    return pl.pallas_call(
        kernel,
        grid=(steps,),
        in_specs=in_specs,
        out_specs=out_specs,
        out_shape=out_shape,
        scratch_shapes=scratch,
        compiler_params=pltpu.CompilerParams(
            dimension_semantics=("arbitrary",), vmem_limit_bytes=56 * 1024 * 1024
        ),
        cost_estimate=pl.CostEstimate(
            flops=flops, bytes_accessed=bytes_accessed, transcendentals=0
        ),
    )


def hot(index, rows, cols, along_rows):
    return jnp.where(
        index == lax.broadcasted_iota(jnp.int32, (rows, cols), along_rows), 1.0, 0.0
    ).astype(BF16)


def norm_kernel(tokens_ref, *refs):
    out_ref = refs[-1]
    out_ref[...] = standardize(tokens_ref[...].astype(F32))[0].astype(BF16)


def norm(tokens, after=()):
    rows, width = tokens.shape
    return call(
        norm_kernel, 1, [whole(rows, width)] + [ANY] * len(after), whole(rows, width),
        shape((rows, width), BF16), 10 * rows * width, 4 * rows * width,
    )(tokens, *after)


def pick_kernel(place_ref, column_ref, *refs):
    out_ref = refs[-1]
    column = column_ref[...].reshape(-1, out_ref.shape[1])
    table = hot(place_ref[...], out_ref.shape[0], column.shape[0], 1)
    out_ref[...] = dot(table, column).astype(BF16)


def pick(place, column, image, after=()):
    count, (depth, _, local_len, width) = place.shape[0], column.shape
    tile, held = min(PICK_TILE, width), depth * local_len
    return call(
        pick_kernel, width // tile,
        [whole(count, 1),
         pl.BlockSpec((depth, 1, local_len, tile), lambda i: (0, image, 0, i))]
        + [ANY] * len(after),
        across(count, tile), shape((count, width), BF16), 2 * count * held * width,
        2 * width * (held + count),
    )(place, column, *after)


def join_kernel(group_ref, *refs):
    halves, out_ref = refs[:-1], refs[-1]
    for i, half in enumerate(halves):

        @pl.when(pl.program_id(0) == i)
        def _():
            out_ref[...] = half[...]


def join(halves, group, size):
    rows, width = halves[0].shape
    return pl.pallas_call(
        join_kernel,
        grid_spec=pltpu.PrefetchScalarGridSpec(
            num_scalar_prefetch=1,
            grid=(len(halves),),
            in_specs=[pl.BlockSpec((rows, width), lambda i, g: (0, 0))] * len(halves),
            out_specs=pl.BlockSpec(
                (rows, width), lambda i, g: (lax.rem(g[0] + i // 2, size) * 2 + lax.rem(i, 2), 0)
            ),
        ),
        out_shape=shape((rows * len(halves), width), BF16),
        compiler_params=pltpu.CompilerParams(
            dimension_semantics=("arbitrary",), vmem_limit_bytes=56 * 1024 * 1024
        ),
        cost_estimate=pl.CostEstimate(
            flops=0, bytes_accessed=4 * rows * len(halves) * width, transcendentals=0
        ),
    )(group.reshape(1), *halves)


def picked_rows(landing_ref, got_refs):
    rows = landing_ref.shape[0] // len(got_refs)
    return [
        dot(hot(landing_ref[b * rows : (b + 1) * rows], rows, got.shape[0], 1), got[...])
        for b, got in enumerate(got_refs)
    ]


def grad_kernel(landing_ref, got0_ref, got1_ref, gate_ref, after_ref, pg_ref, scaled_ref):
    picked = picked_rows(landing_ref, (got0_ref, got1_ref))
    pg_ref[...] = jnp.concatenate(picked, axis=0).astype(BF16)
    scaled_ref[...] = jnp.concatenate(
        [p * gate_ref[b : b + 1, :] for b, p in enumerate(picked)], axis=0
    ).astype(BF16)


def grad_rows(landing, got0, got1, gate, after):
    rows, (count, width), count1 = landing.shape[0], got0.shape, got1.shape[0]
    tile = min(PICK_TILE, width)
    return call(
        grad_kernel, width // tile,
        [whole(rows, 1), across(count, tile), across(count1, tile), across(gate.shape[0], tile),
         ANY],
        [across(rows, tile), across(rows, tile)],
        [shape((rows, width), BF16), shape((rows, width), BF16)],
        2 * rows * width * count, 4 * width * (count + rows),
    )(landing, got0, got1, gate, after)


def expert_kernel(landing_ref, got_ref, scale_ref, shift_ref, w_ref, router_ref, u_ref, after_ref,
                  normed_ref, hidden_ref, d_preact_ref, weighted_ref, d_logit_ref, acc_ref, logit_ref):
    picked = dot(hot(landing_ref[...], landing_ref.shape[0], got_ref.shape[0], 1), got_ref[...])
    normed_ref[...] = picked.astype(BF16)
    hidden = (picked * (1.0 + scale_ref[...]) + shift_ref[...]).astype(BF16)
    hidden_ref[...] = hidden
    term = dot(hidden, w_ref[...])
    logit = jnp.sum(hidden.astype(F32) * router_ref[...], axis=1, keepdims=True)

    @pl.when(pl.program_id(0) == 0)
    def _():
        acc_ref[...] = term
        logit_ref[...] = logit

    @pl.when(pl.program_id(0) > 0)
    def _():
        acc_ref[...] += term
        logit_ref[...] += logit

    @pl.when(pl.program_id(0) == pl.num_programs(0) - 1)
    def _():
        prob = jax.nn.sigmoid(logit_ref[...])
        gelu_value, gelu_slope = gelu_pair(acc_ref[...])
        u = u_ref[...]
        weighted_ref[...] = (prob * gelu_value).astype(BF16)
        d_preact_ref[...] = (prob * u * gelu_slope).astype(BF16)
        d_weight = jnp.sum(gelu_value * u, axis=1, keepdims=True)
        d_logit_ref[...] = (d_weight * prob * (1.0 - prob)).astype(BF16).astype(F32)


def expert(image, landing, got, scale, shift, first_weight, router, u, after):
    rows, (count, width) = landing.shape[0], got.shape
    ff, tile = first_weight.shape[1], min(TILE, width)
    return call(
        expert_kernel, width // tile,
        [whole(rows, 1), across(count, tile), across(1, tile), across(1, tile), along(tile, ff),
         across(1, tile), pl.BlockSpec((rows, ff), lambda i: (image, 0)), ANY],
        [across(rows, tile), across(rows, tile), whole(rows, ff), whole(rows, ff), whole(rows, 1)],
        [shape((rows, width), BF16), shape((rows, width), BF16), shape((rows, ff), BF16),
         shape((rows, ff), BF16), shape((rows, 1), F32)],
        2 * rows * width * (ff + count), 2 * width * (ff + count + 2 * rows),
        [pltpu.VMEM((rows, ff), F32), pltpu.VMEM((rows, 1), F32)],
    )(landing, got, scale, shift, first_weight, router, u, after)


def rows_kernel(landing_ref, d_preact_ref, w_ref, d_logit_ref, router_ref, normed_ref, *refs):
    back_ref, sums_ref = refs[-2:]
    d_rows = dot(d_preact_ref[...], w_ref[...], ((1,), (1,)))
    d_rows += d_logit_ref[...] * router_ref[...]
    table = hot(landing_ref[...], back_ref.shape[0], d_rows.shape[0], 0)
    back_ref[...] = dot(table, d_rows.astype(BF16)).astype(BF16)
    scaled = d_rows * normed_ref[...].astype(F32)
    sums_ref[...] = jnp.concatenate(
        [jnp.sum(v, axis=0, keepdims=True) for v in (d_rows, scaled)], axis=0
    )


def row_grads(landing, d_preact, first_weight, d_logit, router, normed, count, after):
    rows, width = normed.shape
    ff, tile = d_preact.shape[1], min(TILE, width)
    return call(
        rows_kernel, width // tile,
        [whole(1, rows), whole(rows, ff), along(tile, ff), whole(rows, 1), across(1, tile),
         across(rows, tile)] + [ANY] * len(after),
        [across(count, tile), across(2, tile)],
        [shape((count, width), BF16), shape((2, width), F32)],
        2 * rows * width * (ff + count), 2 * width * (ff + count + rows),
    )(landing, d_preact, first_weight, d_logit, router, normed, *after)


def spread_kernel(place_ref, got_ref, *refs):
    out_ref = refs[-1]
    table = hot(place_ref[...], out_ref.shape[0], got_ref.shape[0], 0)
    out_ref[...] = dot(table, got_ref[...]).astype(BF16)


def spread(place, got, held, after=()):
    count, width = got.shape
    tile = min(PICK_TILE, width)
    return call(
        spread_kernel, width // tile, [whole(1, count), across(count, tile)] + [ANY] * len(after),
        across(held, tile), shape((held, width), BF16),
        2 * count * held * width, 2 * width * (held + count),
    )(place, got, *after)


def gate_kernel(weighted0_ref, weighted1_ref, w_ref, grad_ref, after_ref, out_ref):
    half = weighted0_ref.shape[0]
    weighted = jnp.concatenate([weighted0_ref[...], weighted1_ref[...]], axis=0)
    product = dot(weighted, w_ref[...]) * grad_ref[...].astype(F32)
    out_ref[...] = jnp.concatenate(
        [jnp.sum(product[b * half : (b + 1) * half], axis=0, keepdims=True) for b in range(2)],
        axis=0,
    )


def gate_sums(weighted, second_weight, grad, after):
    rows, width = grad.shape
    ff, tile = weighted[0].shape[1], min(PICK_TILE, width)
    return call(
        gate_kernel, width // tile,
        [whole(rows // 2, ff)] * 2 + [across(ff, tile), across(rows, tile), ANY], across(2, tile),
        shape((2, width), F32), 2 * rows * width * ff, 2 * width * (ff + rows),
    )(*weighted, second_weight, grad, after)


def cut_kernel(with_pre, pre_ref, hidden_ref, weighted_ref, after_ref, out_ref):
    parts, rows, total = out_ref.shape
    ff = pre_ref.shape[1] if with_pre else 0
    first, second = hidden_ref.shape[1] // parts, weighted_ref.shape[1] // parts
    used = ff + first + second
    for d in range(parts):
        if with_pre:
            out_ref[d, :, :ff] = pre_ref[...]
        out_ref[d, :, ff : ff + first] = hidden_ref[:, d * first : (d + 1) * first]
        out_ref[d, :, ff + first : used] = weighted_ref[:, d * second : (d + 1) * second]
        if used < total:
            out_ref[d, :, used:] = jnp.zeros((rows, total - used), BF16)


def cut(pre, hidden, weighted, with_pre, parts, after):
    (rows, width), ff = hidden.shape, weighted.shape[1]
    part = (ff if with_pre else 0) + (width + ff) // parts
    part += -part % 128
    return call(
        functools.partial(cut_kernel, with_pre), 1,
        [whole(rows, ff), whole(rows, width), whole(rows, ff), ANY],
        whole(parts, rows, part), shape((parts, rows, part), BF16), 0,
        2 * rows * (width + 2 * ff + parts * part),
    )(pre, hidden, weighted, after)


def outer_kernel(count, left_at, group_ref, *refs):
    left, right, out_ref = refs[: 2 * count], refs[2 * count : -2], refs[-1]
    tall, wide = out_ref.shape
    total = None
    for k in range(count):
        rights = list(right[k * len(right) // count : (k + 1) * len(right) // count])
        rights = [r[...].reshape(-1, wide) for r in rights]
        if len(rights) == 1:
            rights.append(left[2 * k + 1][:, :wide])
        lefts = [left[2 * k + b][:, left_at[b] : left_at[b] + tall] for b in range(2)]
        term = dot(
            jnp.concatenate(lefts, axis=0), jnp.concatenate(rights, axis=0), ((0,), (0,))
        )
        total = term if total is None else total + term
    out_ref[...] = total.astype(BF16)


def outer(sent, left_at, tall, right, group, after):
    (rows, _), count = sent[0].shape, len(sent) // 2
    alone = isinstance(right, list)
    wide = right[0].shape[1] if alone else right.shape[2]
    tile = wide if alone else min(OUTER_TILE, wide)
    right_specs = [pl.BlockSpec((rows, wide), lambda i, g: (0, 0))] * count if alone else [
        pl.BlockSpec(
            (1, rows, tile), lambda i, g, k=k, b=b: (lax.rem(g[0] + count - k, count), b, i)
        )
        for k in range(count)
        for b in range(2)
    ]
    return pl.pallas_call(
        functools.partial(outer_kernel, count, left_at),
        grid_spec=pltpu.PrefetchScalarGridSpec(
            num_scalar_prefetch=1,
            grid=(wide // tile,),
            in_specs=[pl.BlockSpec(p.shape, lambda i, g: (0, 0)) for p in sent]
            + right_specs + [ANY],
            out_specs=pl.BlockSpec((tall, tile), lambda i, g: (0, i)),
        ),
        out_shape=shape((tall, wide), BF16),
        compiler_params=pltpu.CompilerParams(
            dimension_semantics=("arbitrary",), vmem_limit_bytes=56 * 1024 * 1024
        ),
        cost_estimate=pl.CostEstimate(
            flops=4 * rows * count * tall * wide,
            bytes_accessed=2 * (2 * rows * count * (tall + wide) + tall * wide), transcendentals=0,
        ),
    )(group.reshape(1), *sent, *(right if alone else [right] * len(right_specs)), after)


def end_kernel(tokens_ref, grad_ref, *refs):
    out_ref, scale_ref, sum_refs = refs[-1], refs[-2], refs[:-2]
    image = pl.program_id(0)
    normed, inv_std = standardize(tokens_ref[0].astype(F32))
    for b, terms in ((0, sum_refs[:1]), (1, sum_refs[1:])):

        @pl.when(image == b)
        def _():
            d_normed = sum(t[...].astype(F32) for t in terms) * (1.0 + scale_ref[b : b + 1, :])
            inner_mean = jnp.mean(d_normed, axis=-1, keepdims=True)
            cross_mean = jnp.mean(d_normed * normed, axis=-1, keepdims=True)
            out_ref[0] = (
                grad_ref[0].astype(F32)
                + inv_std * (d_normed - inner_mean - normed * cross_mean)
            ).astype(BF16)


def end(tokens, grad, sums, scale):
    images, local_len, width = tokens.shape
    block = pl.BlockSpec((1, local_len, width), lambda i: (i, 0, 0))
    return call(
        end_kernel, images,
        [block] * 2 + [whole(local_len, width)] * len(sums) + [whole(images, width)], block,
        shape(tokens.shape, BF16), 20 * tokens.size, 10 * tokens.size,
    )(tokens, grad, *sums, scale)


def shifted(value, axis, step):
    size = lax.axis_size(axis)
    return lax.ppermute(value, axis, [(i, (i + step) % size) for i in range(size)])


def gather_rows(block, axis):
    size, me = lax.axis_size(axis), lax.axis_index(axis)
    rows = block.shape[0] // 2
    own = [block[:rows], block[rows:]]
    if size == 1:
        return block, own, own
    below = [shifted(h, axis, 1) for h in own]
    above = [shifted(h, axis, -1) for h in own]
    if size == 2:
        return join(own + above, me, size), below, above
    far = [shifted(below[0], axis, 1), shifted(above[1], axis, -1)]
    return join(own + above + far + below, me, size), below + above, far


def swap(blocks, axis):
    size, me = lax.axis_size(axis), lax.axis_index(axis)
    cut = [
        lax.dynamic_index_in_dim(blocks, (me + step) % size, 0, keepdims=False)
        for step in range(size)
    ]
    return [cut[0]] + [shifted(cut[step], axis, step) for step in range(1, size)]


def sum_over(value, axes):
    for axis in axes:
        step = 1
        while step < lax.axis_size(axis):
            value = value + shifted(value, axis, step)
            step *= 2
    return value


def body(tokens, out_grad, steps_ids, ada_weight, router_weight, w_in, w_out, chosen):
    images, local_len, width = tokens.shape
    capacity = chosen.shape[2]
    depth, plane_size = lax.axis_size("z"), lax.axis_size(PLANE)
    groups = lax.axis_size("dp")
    me_z, me_plane = lax.axis_index("z"), lax.axis_index(PLANE)
    expert_id = lax.axis_index(EXPERT)
    rows, held = images * capacity, images * local_len
    slots = min(MOST * depth, capacity)
    count = plane_size * slots

    second_weight, second_near, second_far = gather_rows(w_out[0], "dp")
    first_weight, first_near, first_far = gather_rows(w_in[0], "dp")

    plane_lists = lax.dynamic_slice_in_dim(chosen, me_z * plane_size, plane_size, 0)
    block = plane_lists // local_len
    mine = block % plane_size == me_plane
    place = block // plane_size * local_len + plane_lists % local_len
    rank = jnp.cumsum(mine.astype(jnp.int32), axis=2) - 1
    slot_hot = mine[..., None] & (rank[..., None] == jnp.arange(slots, dtype=jnp.int32))
    places = jnp.sum(jnp.where(slot_hot, place[..., None] + 1, 0), axis=2) - 1
    places = [places[:, b].reshape(count) for b in range(images)]
    own_list = lax.dynamic_index_in_dim(chosen, expert_id, 0, keepdims=False)
    column = own_list // local_len % plane_size
    column_hot = (
        column[..., None] == jnp.arange(plane_size, dtype=jnp.int32)
    ).astype(jnp.int32)
    rank = jnp.sum((jnp.cumsum(column_hot, axis=1) - 1) * column_hot, axis=2)
    landing = (column * slots + rank).reshape(rows)

    sources = depth * plane_size
    home = own_list[0] // local_len
    home_hot = (home[:, None] == jnp.arange(sources, dtype=jnp.int32)).astype(jnp.int32)
    home_rank = jnp.sum((jnp.cumsum(home_hot, axis=0) - 1) * home_hot, axis=1)
    landing_straight = jnp.concatenate([home * MOST + home_rank, landing[capacity:]])
    ours = chosen[:, 0] // local_len == expert_id
    our_rank = jnp.cumsum(ours.astype(jnp.int32), axis=1) - 1
    our_hot = ours[..., None] & (our_rank[..., None] == jnp.arange(MOST, dtype=jnp.int32))
    our_token = (chosen[:, 0] % local_len)[..., None]
    our_place = jnp.sum(jnp.where(our_hot, our_token + 1, 0), axis=1) - 1

    group = lax.axis_index("dp")
    modulation = dot(time_features(steps_ids, ada_weight.shape[0]), ada_weight)
    shift, scale, gate = (modulation[:, i * width : (i + 1) * width] for i in range(3))
    router = lax.dynamic_slice_in_dim(router_weight, expert_id, 1, 1).astype(F32).reshape(1, width)

    def exchange(packed):
        packed = packed.reshape(plane_size, slots, width)
        got = lax.all_to_all(packed, PLANE, split_axis=0, concat_axis=0, tiled=True)
        return got.reshape(count, width)

    def straight(packed):
        packed = packed.reshape(sources, MOST * width // 128, 128)
        got = lax.all_to_all(packed, EXPERT, split_axis=0, concat_axis=0, tiled=True)
        return got.reshape(sources * MOST, width)

    def column_of(value):
        return lax.all_gather(value, "z", axis=0, tiled=False)

    def pack(b, column, image, after):
        return pick(places[b][:, None], column, image, after)

    grad_column1 = column_of(out_grad[1:])
    normed_column0 = column_of(norm(tokens[0])[None])
    normed_column1 = column_of(norm(tokens[1], second_near + [first_near[0], first_near[-1]])[None])
    got_grad0 = straight(pick(our_place.reshape(-1, 1), out_grad[:1][None], 0))
    packed_grad1 = pack(1, grad_column1, 0, [got_grad0] + second_far)
    got_grad1 = exchange(packed_grad1)
    packed_normed0 = pack(
        0, normed_column0, 0, first_near[1:-1] + [packed_grad1]
    )
    got_normed0 = exchange(packed_normed0)
    picked_grad, scaled = grad_rows(
        landing_straight[:, None], got_grad0, got_grad1, gate, packed_normed0
    )
    u = dot(scaled, second_weight, ((1,), (1,)))
    packed_normed1 = pack(1, normed_column1, 0, [u, got_normed0] + first_far)
    got_normed1 = exchange(packed_normed1)
    all_scaled = lax.all_gather(scaled, "dp", axis=0, tiled=False)

    hidden, d_preact, weighted, got_back, sums = [], [], [], [], []
    for b, got in enumerate((got_normed0, got_normed1)):
        own = slice(b * capacity, (b + 1) * capacity)
        normed_b, hidden_b, d_preact_b, weighted_b, d_logit_b = expert(
            b, landing[own, None], got, scale[b : b + 1], shift[b : b + 1], first_weight, router,
            u, packed_normed1 if b == 0 else back_b,
        )
        back_b, sums_b = row_grads(
            landing[None, own], d_preact_b, first_weight, d_logit_b, router, normed_b, count,
            [got_normed1 if b == 0 else got_back[0]],
        )
        for kept, value in zip(
            (hidden, d_preact, weighted, got_back, sums),
            (hidden_b, d_preact_b, weighted_b, exchange(back_b), sums_b),
        ):
            kept.append(value)
    gate_grad = gate_sums(weighted, second_weight, picked_grad, back_b)
    all_preact = [d_preact[0]] + [
        shifted(d_preact[0], "dp", step) for step in range(1, groups)
    ]
    sent = [
        swap(cut(d_preact[b], hidden[b], weighted[b], b == 1, groups, after), "dp")
        for b, after in ((0, d_preact[1]), (1, back_b))
    ]
    part0 = spread(
        places[0][None, :], got_back[0], depth * local_len,
        [d_preact[1], sent[0][1 % groups], sent[0][-1]],
    )
    part1 = spread(
        places[1][None, :], got_back[1], depth * local_len,
        [gate_grad, sent[1][0], sent[0][groups // 2]] + all_preact[1:],
    )
    sums_back = [
        lax.psum_scatter(p, "z", scatter_dimension=0, tiled=True) for p in (part0, part1)
    ]
    d_tokens = end(tokens, out_grad, sums_back, scale)

    d_modulation = sum_over(
        jnp.concatenate(
            [jnp.concatenate([s[i : i + 1] for s in sums], axis=0) for i in range(2)]
            + [gate_grad],
            axis=1,
        ),
        EXPERT,
    )

    pieces = [piece for pair in zip(*sent) for piece in pair]
    ff, first, second = first_weight.shape[1], w_in.shape[1], w_out.shape[1]
    dw_in = outer(pieces, (0, ff), first, all_preact, group, part1)[None]
    dw_out = outer(pieces, (first, ff + first), second, all_scaled, group, part1)[None]
    return (d_tokens, d_modulation, dw_in, dw_out)


def solution(mesh):
    sources, groups = mesh.devices.shape
    fine = Mesh(
        np.asarray(mesh.devices).reshape(sources // 8, 4, 2, groups), ("z", "x", "c", "dp")
    )
    return jax.shard_map(
        body,
        mesh=fine,
        in_specs=(
            P("dp", EXPERT, None),
            P("dp", EXPERT, None),
            P("dp"),
            P(),
            P(),
            P(EXPERT, "dp", None),
            P(EXPERT, "dp", None),
            P(None, "dp", None),
        ),
        out_specs=(
            P("dp", EXPERT, None),
            P("dp", None),
            P(EXPERT, "dp", None),
            P(EXPERT, "dp", None),
        ),
        check_vma=False,
    )
```
